32 devices in a mesh: coarse: 4 (over z), fine: 8 (over y, x, core).
Axes of the slice: x: 2, y: 2, z: 4, core: 2. Of those that a mesh axis runs over, the one named last changes fastest.
Arguments:
- right_side: float32 [64, 4096], P(None, ('coarse', 'fine')), may hold values from -6 to 6
- fine_diagonal: float32 [64, 64, 4096], P(None, None, ('coarse', 'fine'))
- fine_smoother: float32 [64, 64, 4096], P(None, None, ('coarse', 'fine'))
- fine_coupling: float32 [2, 64, 64, 4096], P(None, None, None, ('coarse', 'fine')), may hold values from -0.375 to 0.375
- fine_columns: int32 [2, 4096], P(None, ('coarse', 'fine')), may hold values from 0 to 191, as said below
- send_upward: int32 [1024], P(('coarse', 'fine')), may hold values from 0 to 127, as said below
- send_downward: int32 [1024], P(('coarse', 'fine')), may hold values from 0 to 127, as said below
- prolongation: float32 [64, 64, 4096], P(None, None, ('coarse', 'fine')), may hold values from -0.75 to 0.75
- aggregates: int32 [4096], P(('coarse', 'fine')), may hold values from 0 to 255, as said below
- coarse_diagonal: float32 [64, 64, 1024], P(None, None, ('coarse', 'fine'))
- coarse_smoother: float32 [64, 64, 1024], P(None, None, ('coarse', 'fine'))
- coarse_coupling: float32 [3, 64, 64, 1024], P(None, None, None, ('coarse', 'fine')), may hold values from -0.375 to 0.375
- coarse_columns: int32 [3, 1024], P(None, ('coarse', 'fine')), may hold values from 0 to 255, as said below
Outputs:
- fine_iterate: float32 [64, 4096], P(None, ('coarse', 'fine'))
- coarse_iterate: float32 [64, 1024], P(None, ('coarse', 'fine'))
The draws below stay inside these ranges and needn't reach their ends.
Inputs may be any that keep to these rules, and one draw needn't show every extreme that they name: `fine_columns`: for block row n of device d: values below 32 name the blocks that device d - 1 lists in send_upward, in that order; values 32 to 159 name device d's own blocks in order; larger values name the blocks that device d + 1 lists in send_downward. No slot names the row's own block. Each of the 64 received blocks is named by slot 0 of at least one row of the device. `send_upward`: 32 distinct local block numbers for each device. `send_downward`: 32 distinct local block numbers for each device. aggregates: numbered within the coarse group as f * 32 + j for the j-th coarse block of the group's device f along fine. Every aggregate holds exactly 4 fine blocks, and the blocks of each device name the aggregates of each device of its coarse group exactly 16 times. coarse_columns: numbered within the coarse group as for aggregates; never the row's own block. Among the 96 entries of one device's rows, at most 12 name blocks of any one device of the group, and some device's blocks are named exactly 12 times.
All inputs are finite; a program needn't handle non-finite values.
Results may differ from the reference program's by a relative error of at most 0.0003.
Values sent between devices are 32-bit elements; how exact they have to be, the bound alone decides.
A program may use at most 64 MiB of HBM per device.

```python
import jax
import jax.numpy as jnp
from jax import lax

NODE = 64
BLK_DEV = 128
FINE_NBR = 2
COARSE_NBR = 3
FINE_SWEEPS = 3
COARSE_SWEEPS = 5
AGGREGATE = 4
RIM = 32
CBLK_DEV = 32
PER_OWNER = 16
BLOCKS = 4096
CBLK_GRP = 256
CBLOCKS = 1024
N_COARSE = 4
N_FINE = 8


def with_diagonal(noise, centre):
    eye = (jnp.arange(NODE)[:, None] == jnp.arange(NODE)[None, :]).astype(jnp.float32)
    return centre * eye[:, :, None] + noise


def rim_list(key):
    devices = N_COARSE * N_FINE

    def single(sub):
        first, second = jax.random.split(sub)
        middle = jax.random.permutation(first, BLK_DEV - 2).astype(jnp.int32) + 1
        chosen = jnp.concatenate([jnp.array([0, BLK_DEV - 1], jnp.int32), middle[:RIM - 2]])
        return jax.random.permutation(second, chosen)
    return jax.vmap(single)(jax.random.split(key, devices)).reshape(devices * RIM).astype(jnp.int32)


def draw_fine_diagonal(key, part):
    key = jax.random.fold_in(key, 41)
    noise = jax.random.normal(key, (NODE, NODE, BLOCKS), jnp.float32)
    return with_diagonal(noise * (1.0 / NODE ** 0.5), 4.0)


def draw_fine_smoother(key, part):
    key = jax.random.fold_in(key, 43)
    noise = jax.random.normal(key, (NODE, NODE, BLOCKS), jnp.float32)
    return with_diagonal(noise * (0.075 / NODE ** 0.5), 0.25)


def draw_coarse_diagonal(key, part):
    key = jax.random.fold_in(key, 47)
    noise = jax.random.normal(key, (NODE, NODE, CBLOCKS), jnp.float32)
    return with_diagonal(noise * (1.0 / NODE ** 0.5), 4.0)


def draw_coarse_smoother(key, part):
    key = jax.random.fold_in(key, 53)
    noise = jax.random.normal(key, (NODE, NODE, CBLOCKS), jnp.float32)
    return with_diagonal(noise * (0.075 / NODE ** 0.5), 0.25)


def draw_send_upward(key, part):
    key = jax.random.fold_in(key, 11)
    return rim_list(key)


def draw_send_downward(key, part):
    key = jax.random.fold_in(key, 13)
    return rim_list(key)


def draw_fine_columns(key, part):
    key = jax.random.fold_in(key, 17)
    devices = N_COARSE * N_FINE
    span = BLK_DEV + 2 * RIM

    def single(sub):
        first, second = jax.random.split(sub)
        columns = jax.random.randint(first, (FINE_NBR, BLK_DEV), 0, span, jnp.int32)
        own = RIM + jnp.arange(BLK_DEV, dtype=jnp.int32)
        columns = jnp.where(columns == own[None, :], (columns + 1) % span, columns)
        ordering = jax.random.permutation(second, BLK_DEV)
        rims = jnp.concatenate([jnp.arange(RIM, dtype=jnp.int32), RIM + BLK_DEV + jnp.arange(RIM, dtype=jnp.int32)])
        leading = columns[0].at[ordering[:2 * RIM]].set(rims)
        return columns.at[0].set(leading)
    drawn = jax.vmap(single)(jax.random.split(key, devices))
    return drawn.transpose(1, 0, 2).reshape(FINE_NBR, BLOCKS).astype(jnp.int32)


def draw_aggregates(key, part):
    key = jax.random.fold_in(key, 19)
    first, second = jax.random.split(key)
    count = N_COARSE * N_FINE
    sources = jax.vmap(lambda sub: jax.random.permutation(sub, BLK_DEV))(jax.random.split(first, count))
    sources = sources.reshape(N_COARSE, N_FINE, BLK_DEV).astype(jnp.int32)
    slots = jax.vmap(lambda sub: jax.random.permutation(sub, BLK_DEV))(jax.random.split(second, count))
    slots = slots.reshape(N_COARSE, N_FINE, N_FINE, PER_OWNER).astype(jnp.int32).transpose(0, 2, 1, 3)
    owner_base = (jnp.arange(N_FINE, dtype=jnp.int32) * CBLK_DEV)[None, None, :, None]
    targets = (owner_base + slots // AGGREGATE).reshape(N_COARSE, N_FINE, BLK_DEV)
    inverse = jnp.argsort(sources, axis=-1, stable=True).astype(jnp.int32)
    chosen = jnp.take_along_axis(targets, inverse, axis=-1)
    return chosen.reshape(BLOCKS).astype(jnp.int32)


def draw_coarse_columns(key, part):
    key = jax.random.fold_in(key, 23)
    count = N_COARSE * N_FINE
    fine_pos = jnp.arange(count, dtype=jnp.int32) % N_FINE
    entry = jnp.arange(COARSE_NBR, dtype=jnp.int32)[:, None] * CBLK_DEV + jnp.arange(CBLK_DEV, dtype=jnp.int32)[None, :]
    peers = (fine_pos[None, :, None] + 1 + entry[:, None, :]) % N_FINE
    picks = jax.random.randint(key, (COARSE_NBR, count, CBLK_DEV), 0, CBLK_DEV, jnp.int32)
    rows = jnp.arange(CBLK_DEV, dtype=jnp.int32)[None, None, :]
    clash = (peers == fine_pos[None, :, None]) & (picks == rows)
    picks = jnp.where(clash, (picks + 1) % CBLK_DEV, picks)
    picks = picks.at[0, N_FINE - 1, 0].set(0)
    picks = picks.at[0, N_FINE - 2, 0].set(CBLK_DEV - 1)
    columns = peers * CBLK_DEV + picks
    return columns.reshape(COARSE_NBR, CBLOCKS).astype(jnp.int32)


def block_scale(own_key, dims, pieces, smallest, largest):
    def one(dim, shards_of):
        draws = jax.random.uniform(jax.random.fold_in(jax.random.fold_in(own_key, 6), dim), (shards_of,), jnp.float32, smallest / len(pieces), largest / len(pieces))
        return jnp.repeat(jnp.exp(draws), dims[dim] // shards_of).reshape((-1,) + (1,) * (len(dims) - dim - 1))

    level = one(*pieces[0])
    for cut in pieces[1:]:
        level = level * one(*cut)
    return level


def scatter_about(rng, dims, scale, limit, cuts=(), kind=jnp.bfloat16):
    loudness = block_scale(rng, dims, cuts, -0.22, 0.18) if cuts else 1.0
    values = jax.random.normal(rng, dims, jnp.float32) * scale * loudness
    return jnp.minimum(jnp.maximum(values, -limit), limit).astype(kind)


def setup_inputs(seed: int = 0) -> dict:
    key_of = jax.random.split(jax.random.key(seed), 14)
    right_side = scatter_about(key_of[0], (NODE, BLOCKS), 1.0, 6.0, ((1, 32),), jnp.float32)
    fine_diagonal = draw_fine_diagonal(jax.random.fold_in(key_of[13], 71), 0)
    fine_smoother = draw_fine_smoother(jax.random.fold_in(key_of[13], 71), 0)
    fine_coupling = scatter_about(key_of[3], (FINE_NBR, NODE, NODE, BLOCKS), (4 * NODE) ** -0.5, 0.375, ((3, 32),), jnp.float32)
    fine_columns = draw_fine_columns(jax.random.fold_in(key_of[13], 71), 0)
    send_upward = draw_send_upward(jax.random.fold_in(key_of[13], 71), 0)
    send_downward = draw_send_downward(jax.random.fold_in(key_of[13], 71), 0)
    prolongation = scatter_about(key_of[7], (NODE, NODE, BLOCKS), NODE ** -0.5, 0.75, ((2, 32),), jnp.float32)
    aggregates = draw_aggregates(jax.random.fold_in(key_of[13], 71), 0)
    coarse_diagonal = draw_coarse_diagonal(jax.random.fold_in(key_of[13], 71), 0)
    coarse_smoother = draw_coarse_smoother(jax.random.fold_in(key_of[13], 71), 0)
    coarse_coupling = scatter_about(key_of[11], (COARSE_NBR, NODE, NODE, CBLOCKS), (4 * NODE) ** -0.5, 0.375, ((3, 32),), jnp.float32)
    coarse_columns = draw_coarse_columns(jax.random.fold_in(key_of[13], 71), 0)
    return {"right_side": right_side, "fine_diagonal": fine_diagonal, "fine_smoother": fine_smoother, "fine_coupling": fine_coupling, "fine_columns": fine_columns, "send_upward": send_upward, "send_downward": send_downward, "prolongation": prolongation, "aggregates": aggregates, "coarse_diagonal": coarse_diagonal, "coarse_smoother": coarse_smoother, "coarse_coupling": coarse_coupling, "coarse_columns": coarse_columns}


def apply_blocks(blocks, vector):
    return jnp.einsum("abn,bn->an", blocks, vector, precision=lax.Precision.HIGHEST)


def apply_transposed(blocks, vector):
    return jnp.einsum("abn,an->bn", blocks, vector, precision=lax.Precision.HIGHEST)


def fine_operator(values, fine_diagonal, fine_coupling, fine_columns, send_upward, send_downward):
    devices = N_COARSE * N_FINE
    shaped = values.reshape(NODE, devices, BLK_DEV)
    upward = jnp.take_along_axis(shaped, send_upward.reshape(1, devices, RIM), axis=2)
    downward = jnp.take_along_axis(shaped, send_downward.reshape(1, devices, RIM), axis=2)
    nothing = jnp.zeros((NODE, 1, RIM), values.dtype)
    lower_rim = jnp.concatenate([nothing, upward[:, :-1]], axis=1)
    upper_rim = jnp.concatenate([downward[:, 1:], nothing], axis=1)
    extended = jnp.concatenate([lower_rim, shaped, upper_rim], axis=2)
    summed = apply_blocks(fine_diagonal, values)
    for neighbour in range(FINE_NBR):
        picked = jnp.take_along_axis(extended, fine_columns[neighbour].reshape(1, devices, BLK_DEV), axis=2)
        summed = summed + apply_blocks(fine_coupling[neighbour], picked.reshape(NODE, BLOCKS))
    return summed


def coarse_operator(values, coarse_diagonal, coarse_coupling, coarse_columns):
    shaped = values.reshape(NODE, N_COARSE, CBLK_GRP)
    summed = apply_blocks(coarse_diagonal, values)
    for neighbour in range(COARSE_NBR):
        picked = jnp.take_along_axis(shaped, coarse_columns[neighbour].reshape(1, N_COARSE, CBLK_GRP), axis=2)
        summed = summed + apply_blocks(coarse_coupling[neighbour], picked.reshape(NODE, CBLOCKS))
    return summed


def reference(right_side, fine_diagonal, fine_smoother, fine_coupling, fine_columns, send_upward, send_downward, prolongation, aggregates, coarse_diagonal, coarse_smoother, coarse_coupling, coarse_columns):
    iterate = jnp.zeros((NODE, BLOCKS), jnp.float32)
    for sweep_num in range(FINE_SWEEPS):
        image = fine_operator(iterate, fine_diagonal, fine_coupling, fine_columns, send_upward, send_downward)
        iterate = iterate + apply_blocks(fine_smoother, right_side - image)
    residual = right_side - fine_operator(iterate, fine_diagonal, fine_coupling, fine_columns, send_upward, send_downward)
    pulled = apply_transposed(prolongation, residual)
    group_index = (jnp.arange(BLOCKS, dtype=jnp.int32) // (BLK_DEV * N_FINE)).astype(jnp.int32)
    targets = (group_index * CBLK_GRP + aggregates).astype(jnp.int32)
    coarse_rhs = jax.ops.segment_sum(pulled.T, targets, num_segments=CBLOCKS).T
    correction = jnp.zeros((NODE, CBLOCKS), jnp.float32)
    for sweep_num in range(COARSE_SWEEPS):
        image = coarse_operator(correction, coarse_diagonal, coarse_coupling, coarse_columns)
        correction = correction + apply_blocks(coarse_smoother, coarse_rhs - image)
    return iterate, correction
```

```python
import functools

import jax
import jax.numpy as jnp
from jax import lax
from jax.experimental import pallas as pl
from jax.experimental.pallas import tpu as pltpu
from jax.sharding import PartitionSpec as P

FINE_SWEEPS = 3
COARSE_SWEEPS = 5
MESH = pl.DeviceIdType.MESH
LANES = 128
SUB = 8


def lane_gather(values, index):
    return jnp.take_along_axis(values, index, axis=1)


def sublane_sums(parts):
    row = lax.broadcasted_iota(jnp.int32, (SUB, LANES), 0)
    for bit in (1, 2, 4):
        keep = (row & bit) == 0
        parts = [
            jnp.where(keep, x, y) + pltpu.roll(jnp.where(keep, y, x), SUB - bit, 0)
            for x, y in zip(parts[0::2], parts[1::2])
        ]
    return parts[0]


def product_rows(blocks, vectors, base):
    sums = []
    for a in range(SUB):
        total = None
        for block, vector in zip(blocks, vectors):
            value = block[base + a]
            for s in range(0, value.shape[0], SUB):
                term = value[s : s + SUB] * vector[s : s + SUB]
                total = term if total is None else total + term
        sums.append(total)
    return sublane_sums(sums)


def loop_rows(count, unroll, body):
    def step(i, carry):
        body(pl.multiple_of(i * SUB, SUB))
        return carry

    lax.fori_loop(0, count // SUB, step, 0, unroll=unroll)


def kernel(
    n_coarse, n_fine,
    rs, fd, fs, fc, fcol, su, sd, pr, ag, cd, cs, cc, ccol,
    x_out, y_out,
    rs_v, fd_v, fs_v, fc_v, pr_v, cd_v, cs_v, cc_v,
    packed_op, packed_sm, x_v, ax_v, lower, upper, send_up, send_down,
    onehot, restricted, part_send, part_recv, gathered, gather4, index_v,
    load_sem, chain_send, chain_recv, part_ssem, part_rsem, y_ssem, y_rsem,
):
    c, f = lax.axis_index("coarse"), lax.axis_index("fine")
    node = rs.shape[0]
    groups = LANES // ccol.shape[1]
    width = ccol.shape[1]
    tall = node // groups
    loads = []
    for slot, (src, dst) in enumerate(
        [(rs, rs_v), (fs, fs_v), (fd, fd_v), (fc, fc_v), (pr, pr_v), (cc, cc_v), (cd, cd_v), (cs, cs_v)]
    ):
        load = pltpu.make_async_copy(src, dst, load_sem.at[slot])
        load.start()
        loads.append(load)

    has_lower = jnp.logical_or(c > 0, f > 0)
    has_upper = jnp.logical_or(c < n_coarse - 1, f < n_fine - 1)
    down_id = (jnp.where(f > 0, c, c - 1), jnp.where(f > 0, f - 1, n_fine - 1))
    up_id = (jnp.where(f < n_fine - 1, c, c + 1), jnp.where(f < n_fine - 1, f + 1, 0))

    def peer(t):
        return (c, lax.rem(f + t, n_fine))

    barrier = pltpu.get_barrier_semaphore()

    def greet(t, carry):
        pl.semaphore_signal(barrier, inc=1, device_id=peer(t), device_id_type=MESH)
        return carry

    lax.fori_loop(1, n_fine, greet, 0)
    cross_down = jnp.logical_and(f == 0, c > 0)
    cross_up = jnp.logical_and(f == n_fine - 1, c < n_coarse - 1)

    @pl.when(cross_down)
    def _():
        pl.semaphore_signal(barrier, inc=1, device_id=down_id, device_id_type=MESH)

    @pl.when(cross_up)
    def _():
        pl.semaphore_signal(barrier, inc=1, device_id=up_id, device_id_type=MESH)

    lane16 = lax.broadcasted_iota(jnp.int32, (SUB, LANES), 1)
    lane_group = lane16 // width
    lane_mod = lane16 % width

    index_v[...] = jnp.zeros_like(index_v)
    index_v[0:1, 0:width] = su[...]
    index_v[SUB : SUB + 1, 0:width] = sd[...]
    for k in range(groups - 1):
        index_v[(2 + k) * SUB : (2 + k) * SUB + 1, 0:width] = ccol[k : k + 1, :]

    def spread(k):
        row = jnp.broadcast_to(index_v[k * SUB : k * SUB + 1, :], (SUB, LANES))
        return lane_gather(row, lane_mod)

    up_index, down_index = spread(0), spread(1)
    rim = width
    wanted = f * width + lane_mod
    for k in range(groups - 1):
        wanted = jnp.where(lane_group == k, spread(2 + k), wanted)
    wanted_slot = lax.rem(f - wanted // width + n_fine, n_fine)
    wanted_lane = lax.rem(wanted, width)

    agg = ag[...]
    agg_slot = lax.rem(agg // width - f + n_fine, n_fine) * width + lax.rem(agg, width)

    def hot_rows(t, carry):
        base = pl.multiple_of(t * width, width)
        target = base + lax.broadcasted_iota(jnp.int32, (width, LANES), 0)
        onehot[pl.ds(base, width), :] = (target == agg_slot).astype(jnp.float32).astype(jnp.bfloat16)
        return carry

    lax.fori_loop(0, n_fine, hot_rows, 0)

    @pl.when(jnp.logical_not(has_lower))
    def _():
        lower[...] = jnp.zeros_like(lower)

    @pl.when(jnp.logical_not(has_upper))
    def _():
        upper[...] = jnp.zeros_like(upper)

    loads[0].wait()
    right = rs_v[...]
    loads[1].wait()

    def first_rows(base):
        x_v[pl.ds(base, SUB), :] = product_rows([fs_v], [right], base)

    loop_rows(node, 1, first_rows)

    pl.semaphore_wait(barrier, n_fine - 1 + cross_down.astype(jnp.int32) + cross_up.astype(jnp.int32))

    def up_copy(s):
        return pltpu.make_async_remote_copy(
            send_up.at[s], lower.at[s], chain_send.at[0, s], chain_recv.at[0, s], device_id=up_id, device_id_type=MESH
        )

    def down_copy(s):
        return pltpu.make_async_remote_copy(
            send_down.at[s], upper.at[s], chain_send.at[1, s], chain_recv.at[1, s], device_id=down_id, device_id_type=MESH
        )

    def pack_rows(values, index):
        out = []
        for h in range(0, tall, SUB):
            total = None
            for g in range(groups):
                piece = lane_gather(values[g * tall + h : g * tall + h + SUB], index)
                total = piece if total is None else jnp.where(lane_group == g, piece, total)
            out.append(total)
        return jnp.concatenate(out, axis=0)

    columns = [jnp.broadcast_to(fcol[k : k + 1, :], (SUB, LANES)) for k in range(fcol.shape[0])]
    local = [jnp.clip(col - rim, 0, LANES - 1) for col in columns]
    low = [jnp.clip(col, 0, rim - 1) for col in columns]
    high = [jnp.clip(col - rim - LANES, 0, rim - 1) for col in columns]
    is_low = [col < rim for col in columns]
    is_high = [col >= rim + LANES for col in columns]

    def pack_coarse(part, parts):
        def op_row(a, carry):
            packed_op[a] = jnp.concatenate([cc_v[k, a] for k in range(groups - 1)] + [cd_v[a]], axis=0).T
            return carry

        def sm_row(a, carry):
            packed_sm[a] = jnp.concatenate([cs_v[g * tall + a] for g in range(groups)], axis=0).T
            return carry

        lax.fori_loop(part * node // parts, (part + 1) * node // parts, op_row, 0)
        lax.fori_loop(part * tall // parts, (part + 1) * tall // parts, sm_row, 0)

    parts = 2
    for s in range(FINE_SWEEPS):
        x = x_v[...]
        send_up[s] = pack_rows(x, up_index)
        send_down[s] = pack_rows(x, down_index)

        @pl.when(has_upper)
        def _():
            up_copy(s).start()

        @pl.when(has_lower)
        def _():
            down_copy(s).start()

        if s == 0:
            loads[2].wait()

        def diag_rows(base):
            ax_v[pl.ds(base, SUB), :] = product_rows([fd_v], [x], base)

        loop_rows(node, 1, diag_rows)
        if s == 0:
            loads[3].wait()
        if s == 1:
            for load in loads[5:]:
                load.wait()
        if s >= 1:
            pack_coarse(s - 1, parts)

        @pl.when(has_lower)
        def _():
            up_copy(s).wait_recv()

        @pl.when(has_upper)
        def _():
            down_copy(s).wait_recv()

        picked = []
        for k in range(len(columns)):
            rows = []
            for v in range(node // SUB):
                g, h = v * SUB // tall, v * SUB % tall
                own = lane_gather(x[v * SUB : v * SUB + SUB], local[k])
                below = lane_gather(lower[s, h : h + SUB], low[k] + g * width)
                above = lane_gather(upper[s, h : h + SUB], high[k] + g * width)
                rows.append(jnp.where(is_low[k], below, jnp.where(is_high[k], above, own)))
            picked.append(jnp.concatenate(rows, axis=0))

        def coupling_rows(base):
            at = pl.ds(base, SUB)
            image = product_rows([fc_v.at[k] for k in range(len(columns))], picked, base)
            ax_v[at, :] = rs_v[at, :] - (ax_v[at, :] + image)

        loop_rows(node, 1, coupling_rows)
        if s < FINE_SWEEPS - 1:
            res = ax_v[...]

            def smooth_rows(base):
                at = pl.ds(base, SUB)
                x_v[at, :] = x_v[at, :] + product_rows([fs_v], [res], base)

            loop_rows(node, 1, smooth_rows)
    x_out[...] = x_v[...]

    loads[4].wait()

    def pull_rows(i, total):
        for a in range(SUB):
            total = total + pr_v[i * SUB + a] * ax_v[pl.ds(i * SUB + a, 1), :]
        return total

    pulled = lax.fori_loop(0, node // SUB, pull_rows, jnp.zeros((node, LANES), jnp.float32))
    first = pulled.astype(jnp.bfloat16)
    rest = pulled - first.astype(jnp.float32)
    second = rest.astype(jnp.bfloat16)
    third = (rest - second.astype(jnp.float32)).astype(jnp.bfloat16)
    pieces = jnp.concatenate([first, second, third], axis=0)

    def restrict(q, carry):
        base = pl.multiple_of(q * LANES, LANES)
        table = lax.dot_general(
            pieces, onehot[pl.ds(base, LANES), :], (((1,), (1,)), ((), ())), preferred_element_type=jnp.float32
        )
        table = table[:node] + (table[node : 2 * node] + table[2 * node :])
        for j in range(groups):
            part_send[q * groups + j] = pack_rows(table, j * width + lane_mod)
        return carry

    lax.fori_loop(0, n_fine // groups, restrict, 0)

    def part_copy(t):
        return pltpu.make_async_remote_copy(
            part_send.at[t], part_recv.at[t], part_ssem, part_rsem, device_id=peer(t), device_id_type=MESH
        )

    def part_start(t, carry):
        part_copy(t).start()
        return carry

    lax.fori_loop(1, n_fine, part_start, 0)
    others = pl.ds(1, n_fine - 1)
    part_all = pltpu.make_async_remote_copy(
        part_send.at[others], part_recv.at[others], part_ssem, part_rsem, device_id=peer(1), device_id_type=MESH
    )
    part_all.wait_recv()
    owned = part_send[0]
    owned = lax.fori_loop(1, n_fine, lambda t, total: total + part_recv[t], owned)

    def expand(values):
        return jnp.concatenate(
            [
                lane_gather(values[h : h + SUB], g * width + lane_mod)
                for g in range(groups)
                for h in range(0, tall, SUB)
            ],
            axis=0,
        )

    right4 = expand(owned)

    def smoothed(vector):
        return jnp.concatenate(
            [product_rows([packed_sm], [vector], h) for h in range(0, tall, SUB)], axis=0
        )

    y = smoothed(right4)
    for s in range(COARSE_SWEEPS - 1):
        gathered[s, 0] = y

        def y_copy(t):
            return pltpu.make_async_remote_copy(
                gathered.at[s, 0], gathered.at[s, t], y_ssem.at[s], y_rsem.at[s], device_id=peer(t), device_id_type=MESH
            )

        def y_start(t, carry):
            y_copy(t).start()
            return carry

        lax.fori_loop(1, n_fine, y_start, 0)
        pltpu.make_async_remote_copy(
            gathered.at[s, others], gathered.at[s, others], y_ssem.at[s], y_rsem.at[s],
            device_id=peer(1), device_id_type=MESH,
        ).wait_recv()

        def pick(t, rows):
            mine = wanted_slot == t
            block = gathered[s, t]
            out = []
            for v in range(node // SUB):
                g, h = v * SUB // tall, v * SUB % tall
                piece = lane_gather(block[h : h + SUB], wanted_lane + g * width)
                out.append(jnp.where(mine, piece, rows[v]))
            return tuple(out)

        rows = lax.fori_loop(0, n_fine, pick, tuple(jnp.zeros((SUB, LANES), jnp.float32) for _ in range(node // SUB)))
        vector = jnp.concatenate(rows, axis=0)

        def op_rows(base):
            image = product_rows([packed_op], [vector], base)
            image = image + pltpu.roll(image, 2 * width, 1)
            gather4[pl.ds(base, SUB), :] = image + pltpu.roll(image, width, 1)

        loop_rows(node, 1, op_rows)
        y = y + smoothed(right4 - gather4[...])

    y_out[...] = expand(y)[:, :width]

    for s in range(FINE_SWEEPS):
        @pl.when(has_upper)
        def _():
            up_copy(s).wait_send()

        @pl.when(has_lower)
        def _():
            down_copy(s).wait_send()
    part_all.wait_send()
    for s in range(COARSE_SWEEPS - 1):
        pltpu.make_async_remote_copy(
            gathered.at[s, others], gathered.at[s, others], y_ssem.at[s], y_rsem.at[s],
            device_id=peer(1), device_id_type=MESH,
        ).wait_send()


def body(n_coarse, n_fine, rs, fd, fs, fc, fcol, su, sd, pr, ag, cd, cs, cc, ccol):
    node, blocks = rs.shape
    width = cd.shape[2]
    cd, cs, cc = (jnp.swapaxes(array, -1, -2) for array in (cd, cs, cc))
    groups = LANES // width
    tall = node // groups
    f32 = jnp.float32
    hbm = pl.BlockSpec(memory_space=pl.ANY)
    vmem = pl.BlockSpec(memory_space=pltpu.VMEM)
    sweeps, rounds = FINE_SWEEPS, COARSE_SWEEPS - 1
    return pl.pallas_call(
        functools.partial(kernel, n_coarse, n_fine),
        out_shape=(jax.ShapeDtypeStruct((node, blocks), f32), jax.ShapeDtypeStruct((node, width), f32)),
        in_specs=[hbm, hbm, hbm, hbm, vmem, vmem, vmem, hbm, vmem, hbm, hbm, hbm, vmem],
        out_specs=(vmem, vmem),
        scratch_shapes=[
            pltpu.VMEM(rs.shape, f32),
            pltpu.VMEM(fd.shape, f32),
            pltpu.VMEM(fs.shape, f32),
            pltpu.VMEM(fc.shape, f32),
            pltpu.VMEM(pr.shape, f32),
            pltpu.VMEM(cd.shape, f32),
            pltpu.VMEM(cs.shape, f32),
            pltpu.VMEM(cc.shape, f32),
            pltpu.VMEM((node, node, LANES), f32),
            pltpu.VMEM((tall, node, LANES), f32),
            pltpu.VMEM((node, LANES), f32),
            pltpu.VMEM((node, LANES), f32),
            pltpu.VMEM((sweeps, tall, LANES), f32),
            pltpu.VMEM((sweeps, tall, LANES), f32),
            pltpu.VMEM((sweeps, tall, LANES), f32),
            pltpu.VMEM((sweeps, tall, LANES), f32),
            pltpu.VMEM((n_fine * width, LANES), jnp.bfloat16),
            pltpu.VMEM((node, LANES), f32),
            pltpu.VMEM((n_fine, tall, LANES), f32),
            pltpu.VMEM((n_fine, tall, LANES), f32),
            pltpu.VMEM((rounds, n_fine, tall, LANES), f32),
            pltpu.VMEM((node, LANES), f32),
            pltpu.VMEM(((groups + 1) * SUB, LANES), jnp.int32),
            pltpu.SemaphoreType.DMA((8,)),
            pltpu.SemaphoreType.DMA((2, sweeps)),
            pltpu.SemaphoreType.DMA((2, sweeps)),
            pltpu.SemaphoreType.DMA,
            pltpu.SemaphoreType.DMA,
            pltpu.SemaphoreType.DMA((rounds,)),
            pltpu.SemaphoreType.DMA((rounds,)),
        ],
        compiler_params=pltpu.CompilerParams(
            collective_id=0, has_side_effects=True, vmem_limit_bytes=60 * 1024 * 1024
        ),
    )(rs, fd, fs, fc, fcol, su.reshape(1, -1), sd.reshape(1, -1), pr, ag.reshape(1, -1), cd, cs, cc, ccol)


def solution(mesh):
    blocks = ("coarse", "fine")
    in_specs = (
        P(None, blocks),
        P(None, None, blocks),
        P(None, None, blocks),
        P(None, None, None, blocks),
        P(None, blocks),
        P(blocks),
        P(blocks),
        P(None, None, blocks),
        P(blocks),
        P(None, None, blocks),
        P(None, None, blocks),
        P(None, None, None, blocks),
        P(None, blocks),
    )
    return jax.shard_map(
        functools.partial(body, mesh.shape["coarse"], mesh.shape["fine"]),
        mesh=mesh, in_specs=in_specs, out_specs=(P(None, blocks), P(None, blocks)), check_vma=False,
    )
```

```python
import functools

import jax
import jax.numpy as jnp
from jax import lax
from jax.experimental import pallas as pl
from jax.experimental.pallas import tpu as pltpu
from jax.sharding import PartitionSpec as P

FINE_SWEEPS = 3
COARSE_SWEEPS = 5
MESH = pl.DeviceIdType.MESH
LANES = 128
SUB = 8
UNROLL = 8
OP_SHARES = (0, 10, 23, 36, 50, 64)
SM_SHARES = (0, 6, 11, 16, 16, 16)


def lane_gather(values, index):
    return jnp.take_along_axis(values, index, axis=1)


def sublane_sums(parts):
    row = lax.broadcasted_iota(jnp.int32, (SUB, LANES), 0)
    for bit in (1, 2, 4):
        keep = (row & bit) == 0
        parts = [
            jnp.where(keep, x, y) + pltpu.roll(jnp.where(keep, y, x), SUB - bit, 0)
            for x, y in zip(parts[0::2], parts[1::2])
        ]
    return parts[0]


def product_rows(blocks, vectors, base):
    sums = []
    for a in range(SUB):
        total = None
        for block, vector in zip(blocks, vectors):
            value = block[base + a]
            for s in range(0, value.shape[0], SUB):
                term = value[s : s + SUB] * vector[s : s + SUB]
                total = term if total is None else total + term
        sums.append(total)
    return sublane_sums(sums)


def loop_rows(count, unroll, body):
    def step(i, carry):
        body(pl.multiple_of(i * SUB, SUB))
        return carry

    lax.fori_loop(0, count // SUB, step, 0, unroll=unroll)


def kernel(
    n_coarse, n_fine,
    rs, fd, fs, fc, fcol, su, sd, pr, ag, cd, cs, cc, ccol,
    x_out, y_out,
    rs_v, fd_v, fs_v, fc_v, pr_v, cd_v, cs_v, cc_v,
    packed_op, packed_sm, x_v, ax_v, lower, upper, send_up, send_down,
    onehot, restricted, part_send, part_recv, gathered, gather4, index_v,
    load_sem, chain_send, chain_recv, part_ssem, part_rsem, y_ssem, y_rsem,
):
    c, f = lax.axis_index("coarse"), lax.axis_index("fine")
    node = rs.shape[0]
    groups = LANES // ccol.shape[1]
    width = ccol.shape[1]
    tall = node // groups
    loads = []
    for slot, (src, dst) in enumerate(
        [(rs, rs_v), (fs, fs_v), (fd, fd_v), (fc, fc_v), (cc, cc_v), (cd, cd_v), (cs, cs_v), (pr, pr_v)]
    ):
        load = pltpu.make_async_copy(src, dst, load_sem.at[slot])
        load.start()
        loads.append(load)

    has_lower = jnp.logical_or(c > 0, f > 0)
    has_upper = jnp.logical_or(c < n_coarse - 1, f < n_fine - 1)
    down_id = (jnp.where(f > 0, c, c - 1), jnp.where(f > 0, f - 1, n_fine - 1))
    up_id = (jnp.where(f < n_fine - 1, c, c + 1), jnp.where(f < n_fine - 1, f + 1, 0))

    def peer(m):
        place = f
        for bit in range(n_fine.bit_length() - 1):
            if m >> bit & 1:
                place = place + (1 - 2 * lax.rem(f // 2**bit, 2)) * 2**bit
        return (c, place)

    far_first = range(n_fine - 1, 0, -1)
    peers = [peer(m) for m in range(n_fine)]
    barrier = pltpu.get_barrier_semaphore()

    for m in far_first:
        pl.semaphore_signal(barrier, inc=1, device_id=peers[m], device_id_type=MESH)
    cross_down = jnp.logical_and(f == 0, c > 0)
    cross_up = jnp.logical_and(f == n_fine - 1, c < n_coarse - 1)

    @pl.when(cross_down)
    def _():
        pl.semaphore_signal(barrier, inc=1, device_id=down_id, device_id_type=MESH)

    @pl.when(cross_up)
    def _():
        pl.semaphore_signal(barrier, inc=1, device_id=up_id, device_id_type=MESH)

    lane16 = lax.broadcasted_iota(jnp.int32, (SUB, LANES), 1)
    lane_group = lane16 // width
    lane_mod = lane16 % width

    index_v[...] = jnp.zeros_like(index_v)
    index_v[0:1, 0:width] = su[...]
    index_v[SUB : SUB + 1, 0:width] = sd[...]
    for k in range(groups - 1):
        index_v[(2 + k) * SUB : (2 + k) * SUB + 1, 0:width] = ccol[k : k + 1, :]

    def spread(k):
        row = jnp.broadcast_to(index_v[k * SUB : k * SUB + 1, :], (SUB, LANES))
        return lane_gather(row, lane_mod)

    up_index, down_index = spread(0), spread(1)
    rim = width
    wanted = f * width + lane_mod
    for k in range(groups - 1):
        wanted = jnp.where(lane_group == k, spread(2 + k), wanted)
    wanted_slot = jnp.bitwise_xor(wanted // width, f)
    wanted_lane = lax.rem(wanted, width)

    agg = ag[...]
    agg_slot = jnp.bitwise_xor(agg // width, f) * width + lax.rem(agg, width)

    def hot_rows(t, carry):
        base = pl.multiple_of(t * width, width)
        target = base + lax.broadcasted_iota(jnp.int32, (width, LANES), 0)
        onehot[pl.ds(base, width), :] = (target == agg_slot).astype(jnp.float32).astype(jnp.bfloat16)
        return carry

    lax.fori_loop(0, n_fine, hot_rows, 0)

    @pl.when(jnp.logical_not(has_lower))
    def _():
        lower[...] = jnp.zeros_like(lower)

    @pl.when(jnp.logical_not(has_upper))
    def _():
        upper[...] = jnp.zeros_like(upper)

    loads[0].wait()
    right = rs_v[...]
    loads[1].wait()

    def first_rows(base):
        x_v[pl.ds(base, SUB), :] = product_rows([fs_v], [right], base)

    loop_rows(node, UNROLL, first_rows)

    pl.semaphore_wait(barrier, n_fine - 1 + cross_down.astype(jnp.int32) + cross_up.astype(jnp.int32))

    def up_copy(s):
        return pltpu.make_async_remote_copy(
            send_up.at[s], lower.at[s], chain_send.at[0, s], chain_recv.at[0, s], device_id=up_id, device_id_type=MESH
        )

    def down_copy(s):
        return pltpu.make_async_remote_copy(
            send_down.at[s], upper.at[s], chain_send.at[1, s], chain_recv.at[1, s], device_id=down_id, device_id_type=MESH
        )

    def pack_rows(values, index):
        out = []
        for h in range(0, tall, SUB):
            total = None
            for g in range(groups):
                piece = lane_gather(values[g * tall + h : g * tall + h + SUB], index)
                total = piece if total is None else jnp.where(lane_group == g, piece, total)
            out.append(total)
        return jnp.concatenate(out, axis=0)

    columns = [jnp.broadcast_to(fcol[k : k + 1, :], (SUB, LANES)) for k in range(fcol.shape[0])]
    local = [jnp.clip(col - rim, 0, LANES - 1) for col in columns]
    low = [jnp.clip(col, 0, rim - 1) for col in columns]
    high = [jnp.clip(col - rim - LANES, 0, rim - 1) for col in columns]
    is_low = [col < rim for col in columns]
    is_high = [col >= rim + LANES for col in columns]

    def pack_coarse(part):
        def loop(first, last, step):
            lax.fori_loop(first, last, step, 0, unroll=last - first)

        def op_row(a, carry):
            packed_op[a] = jnp.concatenate([cc_v[k, a] for k in range(groups - 1)] + [cd_v[a]], axis=0).T
            return carry

        def sm_row(a, carry):
            packed_sm[a] = jnp.concatenate([cs_v[g * tall + a] for g in range(groups)], axis=0).T
            return carry

        loop(OP_SHARES[part], OP_SHARES[part + 1], op_row)
        loop(SM_SHARES[part], SM_SHARES[part + 1], sm_row)

    for s in range(FINE_SWEEPS):
        x = x_v[...]
        send_up[s] = pack_rows(x, up_index)

        @pl.when(has_upper)
        def _():
            up_copy(s).start()

        send_down[s] = pack_rows(x, down_index)

        @pl.when(has_lower)
        def _():
            down_copy(s).start()

        if s == 0:
            loads[2].wait()

        def diag_rows(base):
            ax_v[pl.ds(base, SUB), :] = product_rows([fd_v], [x], base)

        loop_rows(node, UNROLL, diag_rows)
        if s == 0:
            loads[3].wait()
            for load in loads[4:7]:
                load.wait()
        pack_coarse(s)

        @pl.when(has_lower)
        def _():
            up_copy(s).wait_recv()

        @pl.when(has_upper)
        def _():
            down_copy(s).wait_recv()

        picked = []
        for k in range(len(columns)):
            rows = []
            for v in range(node // SUB):
                g, h = v * SUB // tall, v * SUB % tall
                own = lane_gather(x[v * SUB : v * SUB + SUB], local[k])
                below = lane_gather(lower[s, h : h + SUB], low[k] + g * width)
                above = lane_gather(upper[s, h : h + SUB], high[k] + g * width)
                rows.append(jnp.where(is_low[k], below, jnp.where(is_high[k], above, own)))
            picked.append(jnp.concatenate(rows, axis=0))

        def coupling_rows(base):
            at = pl.ds(base, SUB)
            image = product_rows([fc_v.at[k] for k in range(len(columns))], picked, base)
            ax_v[at, :] = rs_v[at, :] - (ax_v[at, :] + image)

        loop_rows(node, UNROLL, coupling_rows)
        if s < FINE_SWEEPS - 1:
            res = ax_v[...]

            def smooth_rows(base):
                at = pl.ds(base, SUB)
                x_v[at, :] = x_v[at, :] + product_rows([fs_v], [res], base)

            loop_rows(node, UNROLL, smooth_rows)
    x_out[...] = x_v[...]

    loads[7].wait()

    def pull_rows(i, total):
        for a in range(SUB):
            total = total + pr_v[i * SUB + a] * ax_v[pl.ds(i * SUB + a, 1), :]
        return total

    pulled = lax.fori_loop(0, node // SUB, pull_rows, jnp.zeros((node, LANES), jnp.float32))
    first = pulled.astype(jnp.bfloat16)
    rest = pulled - first.astype(jnp.float32)
    second = rest.astype(jnp.bfloat16)
    third = (rest - second.astype(jnp.float32)).astype(jnp.bfloat16)
    pieces = jnp.concatenate([first, second, third], axis=0)

    def part_copy(m):
        return pltpu.make_async_remote_copy(
            part_send.at[m], part_recv.at[m], part_ssem, part_rsem.at[m], device_id=peers[m], device_id_type=MESH
        )

    for q in reversed(range(n_fine // groups)):
        table = lax.dot_general(
            pieces, onehot[q * LANES : (q + 1) * LANES, :], (((1,), (1,)), ((), ())),
            preferred_element_type=jnp.float32,
        )
        table = table[:node] + (table[node : 2 * node] + table[2 * node :])
        for j in reversed(range(groups)):
            m = q * groups + j
            part_send[m] = pack_rows(table, j * width + lane_mod)
            if m > 0:
                part_copy(m).start()
    pack_coarse(FINE_SWEEPS)
    others = pl.ds(1, n_fine - 1)
    owned = part_send[0]
    for m in range(1, n_fine):
        part_copy(m).wait_recv()
        owned = owned + part_recv[m]

    def expand(values):
        return jnp.concatenate(
            [
                lane_gather(values[h : h + SUB], g * width + lane_mod)
                for g in range(groups)
                for h in range(0, tall, SUB)
            ],
            axis=0,
        )

    right4 = expand(owned)

    def smoothed(vector):
        return jnp.concatenate(
            [product_rows([packed_sm], [vector], h) for h in range(0, tall, SUB)], axis=0
        )

    y = smoothed(right4)
    for s in range(COARSE_SWEEPS - 1):
        gathered[s, 0] = y

        def y_copy(m):
            return pltpu.make_async_remote_copy(
                gathered.at[s, 0], gathered.at[s, m], y_ssem.at[s], y_rsem.at[s, m],
                device_id=peers[m], device_id_type=MESH,
            )

        for m in far_first:
            y_copy(m).start()
        if s == 0:
            pack_coarse(FINE_SWEEPS + 1)
        rows = [None] * (node // SUB)
        for m in range(n_fine):
            if m > 0:
                y_copy(m).wait_recv()
            mine = wanted_slot == m
            for v in range(node // SUB):
                g, h = v * SUB // tall, v * SUB % tall
                piece = lane_gather(gathered[s, m, h : h + SUB], wanted_lane + g * width)
                rows[v] = piece if m == 0 else jnp.where(mine, piece, rows[v])
        vector = jnp.concatenate(rows, axis=0)

        def op_rows(base):
            image = product_rows([packed_op], [vector], base)
            image = image + pltpu.roll(image, 2 * width, 1)
            gather4[pl.ds(base, SUB), :] = image + pltpu.roll(image, width, 1)

        loop_rows(node, UNROLL, op_rows)
        y = y + smoothed(right4 - gather4[...])

    y_out[...] = expand(y).T[:width]

    for s in range(FINE_SWEEPS):
        @pl.when(has_upper)
        def _():
            up_copy(s).wait_send()

        @pl.when(has_lower)
        def _():
            down_copy(s).wait_send()
    pltpu.make_async_remote_copy(
        part_send.at[others], part_recv.at[others], part_ssem, part_rsem.at[1], device_id=peers[1], device_id_type=MESH
    ).wait_send()
    for s in range(COARSE_SWEEPS - 1):
        pltpu.make_async_remote_copy(
            gathered.at[s, others], gathered.at[s, others], y_ssem.at[s], y_rsem.at[s, 1],
            device_id=peers[1], device_id_type=MESH,
        ).wait_send()


def body(n_coarse, n_fine, rs, fd, fs, fc, fcol, su, sd, pr, ag, cd, cs, cc, ccol):
    node, blocks = rs.shape
    width = cd.shape[2]
    cd, cs, cc = (jnp.swapaxes(array, -1, -2) for array in (cd, cs, cc))
    groups = LANES // width
    tall = node // groups
    f32 = jnp.float32
    hbm = pl.BlockSpec(memory_space=pl.ANY)
    vmem = pl.BlockSpec(memory_space=pltpu.VMEM)
    sweeps, rounds = FINE_SWEEPS, COARSE_SWEEPS - 1
    x, y = pl.pallas_call(
        functools.partial(kernel, n_coarse, n_fine),
        out_shape=(jax.ShapeDtypeStruct((node, blocks), f32), jax.ShapeDtypeStruct((width, node), f32)),
        in_specs=[hbm, hbm, hbm, hbm, vmem, vmem, vmem, hbm, vmem, hbm, hbm, hbm, vmem],
        out_specs=(vmem, vmem),
        scratch_shapes=[
            pltpu.VMEM(rs.shape, f32),
            pltpu.VMEM(fd.shape, f32),
            pltpu.VMEM(fs.shape, f32),
            pltpu.VMEM(fc.shape, f32),
            pltpu.VMEM(pr.shape, f32),
            pltpu.VMEM(cd.shape, f32),
            pltpu.VMEM(cs.shape, f32),
            pltpu.VMEM(cc.shape, f32),
            pltpu.VMEM((node, node, LANES), f32),
            pltpu.VMEM((tall, node, LANES), f32),
            pltpu.VMEM((node, LANES), f32),
            pltpu.VMEM((node, LANES), f32),
            pltpu.VMEM((sweeps, tall, LANES), f32),
            pltpu.VMEM((sweeps, tall, LANES), f32),
            pltpu.VMEM((sweeps, tall, LANES), f32),
            pltpu.VMEM((sweeps, tall, LANES), f32),
            pltpu.VMEM((n_fine * width, LANES), jnp.bfloat16),
            pltpu.VMEM((node, LANES), f32),
            pltpu.VMEM((n_fine, tall, LANES), f32),
            pltpu.VMEM((n_fine, tall, LANES), f32),
            pltpu.VMEM((rounds, n_fine, tall, LANES), f32),
            pltpu.VMEM((node, LANES), f32),
            pltpu.VMEM(((groups + 1) * SUB, LANES), jnp.int32),
            pltpu.SemaphoreType.DMA((8,)),
            pltpu.SemaphoreType.DMA((2, sweeps)),
            pltpu.SemaphoreType.DMA((2, sweeps)),
            pltpu.SemaphoreType.DMA,
            pltpu.SemaphoreType.DMA((n_fine,)),
            pltpu.SemaphoreType.DMA((rounds,)),
            pltpu.SemaphoreType.DMA((rounds, n_fine)),
        ],
        compiler_params=pltpu.CompilerParams(
            collective_id=0, has_side_effects=True, vmem_limit_bytes=60 * 1024 * 1024
        ),
    )(rs, fd, fs, fc, fcol, su.reshape(1, -1), sd.reshape(1, -1), pr, ag.reshape(1, -1), cd, cs, cc, ccol)
    return x, y.T


def solution(mesh):
    blocks = ("coarse", "fine")
    in_specs = (
        P(None, blocks),
        P(None, None, blocks),
        P(None, None, blocks),
        P(None, None, None, blocks),
        P(None, blocks),
        P(blocks),
        P(blocks),
        P(None, None, blocks),
        P(blocks),
        P(None, None, blocks),
        P(None, None, blocks),
        P(None, None, None, blocks),
        P(None, blocks),
    )
    return jax.shard_map(
        functools.partial(body, mesh.shape["coarse"], mesh.shape["fine"]),
        mesh=mesh, in_specs=in_specs, out_specs=(P(None, blocks), P(None, blocks)), check_vma=False,
    )
```

```python
import functools

import jax
import jax.numpy as jnp
from jax import lax
from jax.experimental import pallas as pl
from jax.experimental.pallas import tpu as pltpu
from jax.sharding import PartitionSpec as P

FINE_SWEEPS = 3
COARSE_SWEEPS = 5
MESH = pl.DeviceIdType.MESH
LANES = 128
SUB = 8
UNROLL = 8
OP_SHARES = (0, 10, 23, 36, 50, 64)
SM_SHARES = (0, 6, 11, 16, 16, 16)


def lane_gather(values, index):
    return jnp.take_along_axis(values, index, axis=1)


def sublane_sums(parts):
    row = lax.broadcasted_iota(jnp.int32, (SUB, LANES), 0)
    for bit in (1, 2, 4):
        keep = (row & bit) == 0
        parts = [
            jnp.where(keep, x, y) + pltpu.roll(jnp.where(keep, y, x), SUB - bit, 0)
            for x, y in zip(parts[0::2], parts[1::2])
        ]
    return parts[0]


def product_rows(blocks, vectors, base):
    sums = []
    for a in range(SUB):
        total = None
        for block, vector in zip(blocks, vectors):
            value = block[base + a]
            for s in range(0, value.shape[0], SUB):
                term = value[s : s + SUB] * vector[s : s + SUB]
                total = term if total is None else total + term
        sums.append(total)
    return sublane_sums(sums)


def loop_rows(count, unroll, body):
    def step(i, carry):
        body(pl.multiple_of(i * SUB, SUB))
        return carry

    lax.fori_loop(0, count // SUB, step, 0, unroll=unroll)


def kernel(
    n_coarse, n_fine,
    rs, fd, fs, fc, fcol, su, sd, pr, ag, cd, cs, cc, ccol,
    x_out, y_out,
    rs_v, fd_v, fs_v, fc_v, pr_v, cd_v, cs_v, cc_v,
    packed_op, packed_sm, x_v, ax_v, lower, upper, send_up, send_down,
    onehot, restricted, part_send, part_recv, gathered, gather4, index_v,
    load_sem, chain_send, chain_recv, part_ssem, part_rsem, y_ssem, y_rsem,
):
    c, f = lax.axis_index("coarse"), lax.axis_index("fine")
    node = rs.shape[0]
    groups = LANES // ccol.shape[1]
    width = ccol.shape[1]
    tall = node // groups
    loads = []
    for slot, (src, dst) in enumerate(
        [(rs, rs_v), (fs, fs_v), (fd, fd_v), (fc, fc_v), (cc, cc_v), (cd, cd_v), (cs, cs_v), (pr, pr_v)]
    ):
        load = pltpu.make_async_copy(src, dst, load_sem.at[slot])
        load.start()
        loads.append(load)

    has_lower = jnp.logical_or(c > 0, f > 0)
    has_upper = jnp.logical_or(c < n_coarse - 1, f < n_fine - 1)
    down_id = (jnp.where(f > 0, c, c - 1), jnp.where(f > 0, f - 1, n_fine - 1))
    up_id = (jnp.where(f < n_fine - 1, c, c + 1), jnp.where(f < n_fine - 1, f + 1, 0))

    def peer(m):
        place = f
        for bit in range(n_fine.bit_length() - 1):
            if m >> bit & 1:
                place = place + (1 - 2 * lax.rem(f // 2**bit, 2)) * 2**bit
        return (c, place)

    far_first = range(n_fine - 1, 0, -1)
    peers = [peer(m) for m in range(n_fine)]
    barrier = pltpu.get_barrier_semaphore()

    for m in far_first:
        pl.semaphore_signal(barrier, inc=1, device_id=peers[m], device_id_type=MESH)
    cross_down = jnp.logical_and(f == 0, c > 0)
    cross_up = jnp.logical_and(f == n_fine - 1, c < n_coarse - 1)

    @pl.when(cross_down)
    def _():
        pl.semaphore_signal(barrier, inc=1, device_id=down_id, device_id_type=MESH)

    @pl.when(cross_up)
    def _():
        pl.semaphore_signal(barrier, inc=1, device_id=up_id, device_id_type=MESH)

    lane16 = lax.broadcasted_iota(jnp.int32, (SUB, LANES), 1)
    lane_group = lane16 // width
    lane_mod = lane16 % width

    index_v[...] = jnp.zeros_like(index_v)
    index_v[0:1, 0:width] = su[...]
    index_v[SUB : SUB + 1, 0:width] = sd[...]
    for k in range(groups - 1):
        index_v[(2 + k) * SUB : (2 + k) * SUB + 1, 0:width] = ccol[k : k + 1, :]

    def spread(k):
        row = jnp.broadcast_to(index_v[k * SUB : k * SUB + 1, :], (SUB, LANES))
        return lane_gather(row, lane_mod)

    up_index, down_index = spread(0), spread(1)
    rim = width
    wanted = f * width + lane_mod
    for k in range(groups - 1):
        wanted = jnp.where(lane_group == k, spread(2 + k), wanted)
    wanted_slot = jnp.bitwise_xor(wanted // width, f)
    wanted_lane = lax.rem(wanted, width)

    agg = ag[...]
    agg_slot = jnp.bitwise_xor(agg // width, f) * width + lax.rem(agg, width)

    def hot_rows(t, carry):
        base = pl.multiple_of(t * width, width)
        target = base + lax.broadcasted_iota(jnp.int32, (width, LANES), 0)
        onehot[pl.ds(base, width), :] = (target == agg_slot).astype(jnp.float32).astype(jnp.bfloat16)
        return carry

    lax.fori_loop(0, n_fine, hot_rows, 0)

    @pl.when(jnp.logical_not(has_lower))
    def _():
        lower[...] = jnp.zeros_like(lower)

    @pl.when(jnp.logical_not(has_upper))
    def _():
        upper[...] = jnp.zeros_like(upper)

    loads[0].wait()
    right = rs_v[...]
    loads[1].wait()

    def first_rows(base):
        x_v[pl.ds(base, SUB), :] = product_rows([fs_v], [right], base)

    loop_rows(node, UNROLL, first_rows)

    pl.semaphore_wait(barrier, n_fine - 1 + cross_down.astype(jnp.int32) + cross_up.astype(jnp.int32))

    def up_copy(s):
        return pltpu.make_async_remote_copy(
            send_up.at[s], lower.at[s], chain_send.at[0, s], chain_recv.at[0, s], device_id=up_id, device_id_type=MESH
        )

    def down_copy(s):
        return pltpu.make_async_remote_copy(
            send_down.at[s], upper.at[s], chain_send.at[1, s], chain_recv.at[1, s], device_id=down_id, device_id_type=MESH
        )

    def pack_rows(values, index):
        out = []
        for h in range(0, tall, SUB):
            total = None
            for g in range(groups):
                piece = lane_gather(values[g * tall + h : g * tall + h + SUB], index)
                total = piece if total is None else jnp.where(lane_group == g, piece, total)
            out.append(total)
        return jnp.concatenate(out, axis=0)

    columns = [jnp.broadcast_to(fcol[k : k + 1, :], (SUB, LANES)) for k in range(fcol.shape[0])]
    local = [jnp.clip(col - rim, 0, LANES - 1) for col in columns]
    low = [jnp.clip(col, 0, rim - 1) for col in columns]
    high = [jnp.clip(col - rim - LANES, 0, rim - 1) for col in columns]
    is_low = [col < rim for col in columns]
    is_high = [col >= rim + LANES for col in columns]

    def pack_coarse(part):
        def loop(first, last, step):
            lax.fori_loop(first, last, step, 0, unroll=last - first)

        def op_row(a, carry):
            packed_op[a] = jnp.concatenate([cc_v[k, a] for k in range(groups - 1)] + [cd_v[a]], axis=0).T
            return carry

        def sm_row(a, carry):
            packed_sm[a] = jnp.concatenate([cs_v[g * tall + a] for g in range(groups)], axis=0).T
            return carry

        loop(OP_SHARES[part], OP_SHARES[part + 1], op_row)
        loop(SM_SHARES[part], SM_SHARES[part + 1], sm_row)

    for s in range(FINE_SWEEPS):
        x = x_v[...]
        send_up[s] = pack_rows(x, up_index)

        @pl.when(has_upper)
        def _():
            up_copy(s).start()

        send_down[s] = pack_rows(x, down_index)

        @pl.when(has_lower)
        def _():
            down_copy(s).start()

        if s == 0:
            loads[2].wait()

        def diag_rows(base):
            ax_v[pl.ds(base, SUB), :] = product_rows([fd_v], [x], base)

        loop_rows(node, UNROLL, diag_rows)
        if s == 0:
            loads[3].wait()
            for load in loads[4:7]:
                load.wait()
        pack_coarse(s)

        @pl.when(has_lower)
        def _():
            up_copy(s).wait_recv()

        @pl.when(has_upper)
        def _():
            down_copy(s).wait_recv()

        picked = []
        for k in range(len(columns)):
            rows = []
            for v in range(node // SUB):
                g, h = v * SUB // tall, v * SUB % tall
                own = lane_gather(x[v * SUB : v * SUB + SUB], local[k])
                below = lane_gather(lower[s, h : h + SUB], low[k] + g * width)
                above = lane_gather(upper[s, h : h + SUB], high[k] + g * width)
                rows.append(jnp.where(is_low[k], below, jnp.where(is_high[k], above, own)))
            picked.append(jnp.concatenate(rows, axis=0))

        def coupling_rows(base):
            at = pl.ds(base, SUB)
            image = product_rows([fc_v.at[k] for k in range(len(columns))], picked, base)
            ax_v[at, :] = rs_v[at, :] - (ax_v[at, :] + image)

        loop_rows(node, UNROLL, coupling_rows)
        if s < FINE_SWEEPS - 1:
            res = ax_v[...]

            def smooth_rows(base):
                at = pl.ds(base, SUB)
                x_v[at, :] = x_v[at, :] + product_rows([fs_v], [res], base)

            loop_rows(node, UNROLL, smooth_rows)
    x_out[...] = x_v[...]

    loads[7].wait()

    def pull_rows(i, total):
        for a in range(SUB):
            total = total + pr_v[i * SUB + a] * ax_v[pl.ds(i * SUB + a, 1), :]
        return total

    pulled = lax.fori_loop(0, node // SUB, pull_rows, jnp.zeros((node, LANES), jnp.float32))
    first = pulled.astype(jnp.bfloat16)
    rest = pulled - first.astype(jnp.float32)
    second = rest.astype(jnp.bfloat16)
    third = (rest - second.astype(jnp.float32)).astype(jnp.bfloat16)
    pieces = jnp.concatenate([first, second, third], axis=0)

    def part_copy(m):
        return pltpu.make_async_remote_copy(
            part_send.at[m], part_recv.at[m], part_ssem, part_rsem.at[m], device_id=peers[m], device_id_type=MESH
        )

    for q in reversed(range(n_fine // groups)):
        table = lax.dot_general(
            pieces, onehot[q * LANES : (q + 1) * LANES, :], (((1,), (1,)), ((), ())),
            preferred_element_type=jnp.float32,
        )
        table = table[:node] + (table[node : 2 * node] + table[2 * node :])
        for j in reversed(range(groups)):
            m = q * groups + j
            part_send[m] = pack_rows(table, j * width + lane_mod)
            if m > 0:
                part_copy(m).start()
    pack_coarse(FINE_SWEEPS)
    others = pl.ds(1, n_fine - 1)
    owned = part_send[0]
    for m in range(1, n_fine):
        part_copy(m).wait_recv()
        owned = owned + part_recv[m]

    def expand(values):
        return jnp.concatenate(
            [
                lane_gather(values[h : h + SUB], g * width + lane_mod)
                for g in range(groups)
                for h in range(0, tall, SUB)
            ],
            axis=0,
        )

    right4 = expand(owned)

    def smoothed(vector):
        return jnp.concatenate(
            [product_rows([packed_sm], [vector], h) for h in range(0, tall, SUB)], axis=0
        )

    y = smoothed(right4)
    for s in range(COARSE_SWEEPS - 1):
        gathered[s, 0] = y

        def y_copy(m):
            return pltpu.make_async_remote_copy(
                gathered.at[s, 0], gathered.at[s, m], y_ssem.at[s], y_rsem.at[s, m],
                device_id=peers[m], device_id_type=MESH,
            )

        for m in far_first:
            y_copy(m).start()
        if s == 0:
            pack_coarse(FINE_SWEEPS + 1)
        rows = [None] * (node // SUB)
        for m in range(n_fine):
            if m > 0:
                y_copy(m).wait_recv()
            mine = wanted_slot == m
            for v in range(node // SUB):
                g, h = v * SUB // tall, v * SUB % tall
                piece = lane_gather(gathered[s, m, h : h + SUB], wanted_lane + g * width)
                rows[v] = piece if m == 0 else jnp.where(mine, piece, rows[v])
        vector = jnp.concatenate(rows, axis=0)

        def op_rows(base):
            image = product_rows([packed_op], [vector], base)
            image = image + pltpu.roll(image, 2 * width, 1)
            gather4[pl.ds(base, SUB), :] = image + pltpu.roll(image, width, 1)

        loop_rows(node, UNROLL, op_rows)
        y = y + smoothed(right4 - gather4[...])

    y_out[...] = expand(y).T[:width]

    for s in range(FINE_SWEEPS):
        @pl.when(has_upper)
        def _():
            up_copy(s).wait_send()

        @pl.when(has_lower)
        def _():
            down_copy(s).wait_send()
    pltpu.make_async_remote_copy(
        part_send.at[others], part_recv.at[others], part_ssem, part_rsem.at[1], device_id=peers[1], device_id_type=MESH
    ).wait_send()
    for s in range(COARSE_SWEEPS - 1):
        pltpu.make_async_remote_copy(
            gathered.at[s, others], gathered.at[s, others], y_ssem.at[s], y_rsem.at[s, 1],
            device_id=peers[1], device_id_type=MESH,
        ).wait_send()


def place_results(x, y, x_out, y_out):
    x_out[...] = x[...]
    y_out[...] = y[...]


def body(n_coarse, n_fine, rs, fd, fs, fc, fcol, su, sd, pr, ag, cd, cs, cc, ccol):
    node, blocks = rs.shape
    width = cd.shape[2]
    cd, cs, cc = (jnp.swapaxes(array, -1, -2) for array in (cd, cs, cc))
    groups = LANES // width
    tall = node // groups
    f32 = jnp.float32
    hbm = pl.BlockSpec(memory_space=pl.ANY)
    vmem = pl.BlockSpec(memory_space=pltpu.VMEM)
    sweeps, rounds = FINE_SWEEPS, COARSE_SWEEPS - 1
    x, y = pl.pallas_call(
        functools.partial(kernel, n_coarse, n_fine),
        out_shape=(jax.ShapeDtypeStruct((node, blocks), f32), jax.ShapeDtypeStruct((width, node), f32)),
        in_specs=[hbm, hbm, hbm, hbm, vmem, vmem, vmem, hbm, vmem, hbm, hbm, hbm, vmem],
        out_specs=(vmem, vmem),
        scratch_shapes=[
            pltpu.VMEM(rs.shape, f32),
            pltpu.VMEM(fd.shape, f32),
            pltpu.VMEM(fs.shape, f32),
            pltpu.VMEM(fc.shape, f32),
            pltpu.VMEM(pr.shape, f32),
            pltpu.VMEM(cd.shape, f32),
            pltpu.VMEM(cs.shape, f32),
            pltpu.VMEM(cc.shape, f32),
            pltpu.VMEM((node, node, LANES), f32),
            pltpu.VMEM((tall, node, LANES), f32),
            pltpu.VMEM((node, LANES), f32),
            pltpu.VMEM((node, LANES), f32),
            pltpu.VMEM((sweeps, tall, LANES), f32),
            pltpu.VMEM((sweeps, tall, LANES), f32),
            pltpu.VMEM((sweeps, tall, LANES), f32),
            pltpu.VMEM((sweeps, tall, LANES), f32),
            pltpu.VMEM((n_fine * width, LANES), jnp.bfloat16),
            pltpu.VMEM((node, LANES), f32),
            pltpu.VMEM((n_fine, tall, LANES), f32),
            pltpu.VMEM((n_fine, tall, LANES), f32),
            pltpu.VMEM((rounds, n_fine, tall, LANES), f32),
            pltpu.VMEM((node, LANES), f32),
            pltpu.VMEM(((groups + 1) * SUB, LANES), jnp.int32),
            pltpu.SemaphoreType.DMA((8,)),
            pltpu.SemaphoreType.DMA((2, sweeps)),
            pltpu.SemaphoreType.DMA((2, sweeps)),
            pltpu.SemaphoreType.DMA,
            pltpu.SemaphoreType.DMA((n_fine,)),
            pltpu.SemaphoreType.DMA((rounds,)),
            pltpu.SemaphoreType.DMA((rounds, n_fine)),
        ],
        compiler_params=pltpu.CompilerParams(
            collective_id=0, has_side_effects=True, vmem_limit_bytes=60 * 1024 * 1024
        ),
    )(rs, fd, fs, fc, fcol, su.reshape(1, -1), sd.reshape(1, -1), pr, ag.reshape(1, -1), cd, cs, cc, ccol)
    x, y = pl.pallas_call(
        place_results,
        out_shape=(jax.ShapeDtypeStruct(x.shape, f32), jax.ShapeDtypeStruct(y.shape, f32)),
        in_specs=[vmem, vmem],
        out_specs=(vmem, vmem),
    )(x, y)
    return x, y.T


def solution(mesh):
    blocks = ("coarse", "fine")
    in_specs = (
        P(None, blocks),
        P(None, None, blocks),
        P(None, None, blocks),
        P(None, None, None, blocks),
        P(None, blocks),
        P(blocks),
        P(blocks),
        P(None, None, blocks),
        P(blocks),
        P(None, None, blocks),
        P(None, None, blocks),
        P(None, None, None, blocks),
        P(None, blocks),
    )
    return jax.shard_map(
        functools.partial(body, mesh.shape["coarse"], mesh.shape["fine"]),
        mesh=mesh, in_specs=in_specs, out_specs=(P(None, blocks), P(None, blocks)), check_vma=False,
    )
```
